32 devices in a mesh: req: 8 (over y, x, core), mlp: 4 (over z).
Axes of the slice: x: 2, y: 2, z: 4, core: 2. Of those that a mesh axis runs over, the one named last changes fastest.
Arguments:
- tokens: bfloat16 [2048, 2560], P('req'), may hold values from -125 to 125
- lengths: int32 [8, 4], P('req'), may hold values from 1 to 128, 256 in all within a row
- page_table: int32 [8, 16], P('req'), may hold values from 0 to 15, each once within a row
- attn_norm: float32 [2560], replicated, may hold values from 0.25 to 1.75
- qkv_weight: bfloat16 [2560, 8, 768], P(None, 'mlp'), may hold values from -0.125 to 0.125
- q_norm: float32 [128], replicated, may hold values from 0.25 to 1.75
- k_norm: float32 [128], replicated, may hold values from 0.25 to 1.75
- o_weight: bfloat16 [4096, 2560], P('mlp'), may hold values from -0.09375 to 0.09375
- mlp_norm: float32 [2560], replicated, may hold values from 0.25 to 1.75
- gate_up: bfloat16 [9728, 2, 2560], P(('req', 'mlp')), may hold values from -0.125 to 0.125
- down_weight: bfloat16 [9728, 2560], P(('req', 'mlp')), may hold values from -0.0625 to 0.0625
Outputs:
- layer_out: bfloat16 [2048, 2560], P(('req', 'mlp'))
- kv_cache: bfloat16 [2, 128, 16, 8, 128], P(None, 'req', None, 'mlp')
The draws below stay inside these ranges and needn't reach their ends.
Inputs may be any that keep to these rules, and one draw needn't show every extreme that they name: `lengths`: each row sums to 256, and the longest prompt of every pack is exactly 128. `page_table`: each row is a permutation of 0 .. 15.
All inputs are finite; a program needn't handle non-finite values.
Results may differ from the reference program's by a relative error of at most 0.0049.
Values may be sent and summed in bfloat16 or wider, within the bound.
A program may use at most 128 MiB of HBM per device.

```python
import math
import jax
import jax.numpy as jnp
import numpy as np
from jax import lax

D = 2560
H = 32
KV = 8
HD = 128
FF = 9728
SEQS = 4
PAGE = 16
GQ = 4
SLOTS = 256
LONGEST = 128
PAGES = 16
GROUPS = 8
TOKENS = 2048


def draw_tokens(key, part):
    key_base, key_rows, key_cols = jax.random.split(key, 3)
    row_scale = jnp.exp(jax.random.uniform(key_rows, (TOKENS, 1), jnp.float32, 0.0, math.log(10.0)))
    col_scale = jnp.exp(jax.random.uniform(key_cols, (1, D), jnp.float32, 0.0, math.log(10.0)))
    base = jnp.clip(jax.random.normal(key_base, (TOKENS, D), jnp.float32), -5.0, 5.0)
    return (base * row_scale * col_scale / 4.0).astype(jnp.bfloat16)


def level_of(stream_key, dims, cuts, smallest, top_value):
    level, own = 1.0, jax.random.fold_in(stream_key, 6)
    for dim, shards_of in cuts:
        heights = jnp.exp(jax.random.uniform(jax.random.fold_in(own, dim), (shards_of,), jnp.float32, smallest / len(cuts), top_value / len(cuts)))
        level = level * jnp.repeat(heights, dims[dim] // shards_of).reshape([-1 if axis == dim else 1 for axis in range(len(dims))])
    return level


def length_profile(count, total, limit, slope):
    portions = [(1 << 20) // math.isqrt(rank ** slope) + 1 for rank in range(2, count + 1)]
    rest, given = total - limit - (count - 1), [1] * (count - 1)
    while rest > 0:
        free = [i for i in range(count - 1) if given[i] < limit]
        mass, budget = sum([portions[i] for i in free]), rest
        for i in free:
            extra = min(limit - given[i], max(1, budget * portions[i] // mass), rest)
            given[i] = given[i] + extra
            rest = rest - extra
    return np.array([limit] + given)


def ragged(rng, count, total, most, lean):
    if count == 2:
        one = jax.random.randint(rng, (), max(1, total - most), min(most, total - 1) + 1)
        return jnp.stack([one, total - one])
    sizes = jnp.asarray(length_profile(count, total, most, lean), jnp.int32)
    twos = (count - 1) // 2
    giver, taker = sizes[1:1 + 2 * twos:2], sizes[2:2 + 2 * twos:2]
    slack = jnp.minimum(giver - 1, most - taker)
    moved = jax.random.randint(jax.random.fold_in(rng, 1), (twos,), 0, 1 << 20) % (slack + 1)
    sizes = sizes.at[1:1 + 2 * twos:2].set(giver - moved).at[2:2 + 2 * twos:2].set(taker + moved)
    return sizes[jax.random.permutation(jax.random.fold_in(rng, 2), count)]


def centred(stream_key, shape, spread, most, cuts=(), kind=jnp.bfloat16):
    result = spread * jax.random.normal(stream_key, shape, jnp.float32)
    if cuts:
        result = result * level_of(stream_key, shape, cuts, -0.22, 0.18)
    return jnp.clip(result, -most, most).astype(kind)


def setup_inputs(seed: int = 0) -> dict:
    splits = jax.random.split(jax.random.key(seed), 12)
    return {
        "tokens": draw_tokens(jax.random.fold_in(splits[11], 71), 0),
        "lengths": jax.vmap(lambda own: ragged(own, SEQS, SLOTS, LONGEST, 2))(jax.random.split(splits[1], GROUPS)).reshape((GROUPS, SEQS)).astype(jnp.int32),
        "page_table": jax.vmap(lambda own: jax.random.permutation(own, PAGES))(jax.random.split(splits[2], GROUPS)).reshape((GROUPS, PAGES)).astype(jnp.int32),
        "attn_norm": jnp.clip(1.0 + 0.15 * jax.random.normal(splits[3], (D,), jnp.float32), 0.25, 1.75),
        "qkv_weight": centred(splits[4], (D, KV, (GQ + 2) * HD), D ** -0.5, 0.125, ((1, 4),)),
        "q_norm": jnp.clip(1.0 + 0.15 * jax.random.normal(splits[5], (HD,), jnp.float32), 0.25, 1.75),
        "k_norm": jnp.clip(1.0 + 0.15 * jax.random.normal(splits[6], (HD,), jnp.float32), 0.25, 1.75),
        "o_weight": centred(splits[7], (H * HD, D), (H * HD) ** -0.5, 0.09375, ((0, 4),)),
        "mlp_norm": jnp.clip(1.0 + 0.15 * jax.random.normal(splits[8], (D,), jnp.float32), 0.25, 1.75),
        "gate_up": centred(splits[9], (FF, 2, D), D ** -0.5, 0.125, ((0, 32),)),
        "down_weight": centred(splits[10], (FF, D), FF ** -0.5, 0.0625, ((0, 32),)),
    }


rope_theta = 1000000.0
norm_eps = 1e-06

def rms_scale(values, gain):
    mean_sq = lax.optimization_barrier(jnp.mean(values * values, axis=-1, keepdims=True))
    return values * lax.rsqrt(mean_sq + norm_eps) * gain

def positions_of(lengths, slots):
    ends = jnp.cumsum(lengths).astype(jnp.int32)
    slot_ids = jnp.arange(slots, dtype=jnp.int32)
    passed = (ends[None, :] <= slot_ids[:, None]).astype(jnp.int32)
    segment = lax.optimization_barrier(jnp.sum(passed, axis=1)).astype(jnp.int32)
    start = lax.optimization_barrier(jnp.sum(passed * lengths[None, :], axis=1)).astype(jnp.int32)
    return (slot_ids, segment, slot_ids - start)

def rotate(values, position, head_dim):
    half = head_dim // 2
    freq = rope_theta ** (-(2.0 * jnp.arange(half, dtype=jnp.float32)) / head_dim)
    angle = position.astype(jnp.float32)[:, None] * freq[None, :]
    shape = (angle.shape[0],) + (1,) * (values.ndim - 2) + (half,)
    cosine = jnp.cos(angle).reshape(shape)
    sine = jnp.sin(angle).reshape(shape)
    first = values[..., :half]
    second = values[..., half:]
    return jnp.concatenate([first * cosine - second * sine, second * cosine + first * sine], axis=-1)

def reference(tokens, lengths, page_table, attn_norm, qkv_weight, q_norm, k_norm, o_weight, mlp_norm, gate_up, down_weight):
    packed = tokens.reshape(GROUPS, SLOTS, D)

    def one_group(items):
        rows, lens, pages = items
        slot_ids, segment, position = positions_of(lens, SLOTS)
        normed = rms_scale(rows.astype(jnp.float32), attn_norm).astype(jnp.bfloat16)
        qkv = jnp.dot(normed, qkv_weight.reshape(D, KV * (GQ + 2) * HD), preferred_element_type=jnp.float32)
        qkv = qkv.reshape(SLOTS, KV, (GQ + 2) * HD)
        query = qkv[:, :, :GQ * HD].reshape(SLOTS, KV, GQ, HD)
        key = qkv[:, :, GQ * HD:(GQ + 1) * HD]
        value = qkv[:, :, (GQ + 1) * HD:]
        query = rotate(rms_scale(query, q_norm), position, HD).astype(jnp.bfloat16)
        key = rotate(rms_scale(key, k_norm), position, HD).astype(jnp.bfloat16)
        value = value.astype(jnp.bfloat16)
        key_pages = key.reshape(PAGES, PAGE, KV, HD)
        value_pages = value.reshape(PAGES, PAGE, KV, HD)
        cache = jnp.zeros((2, PAGES, PAGE, KV, HD), jnp.bfloat16).at[:, pages].set(jnp.stack([key_pages, value_pages]))
        scores = jnp.einsum('skgd,tkd->kgst', query.astype(jnp.float32), key.astype(jnp.float32)) / math.sqrt(HD)
        allowed = (segment[:, None] == segment[None, :]) & (slot_ids[None, :] <= slot_ids[:, None])
        weights = jnp.where(allowed, jnp.exp(scores), 0.0)
        probs = (weights / lax.optimization_barrier(jnp.sum(weights, axis=-1, keepdims=True))).astype(jnp.bfloat16)
        context = jnp.einsum('kgst,tkd->skgd', probs.astype(jnp.float32), value.astype(jnp.float32))
        context = context.astype(jnp.bfloat16).reshape(SLOTS, H * HD)
        attn_out = jnp.dot(context, o_weight, preferred_element_type=jnp.float32)
        resid = rows.astype(jnp.float32) + attn_out
        mlp_in = rms_scale(resid, mlp_norm).astype(jnp.bfloat16)
        gate = jnp.dot(mlp_in, gate_up[:, 0, :].T, preferred_element_type=jnp.float32)
        upper = jnp.dot(mlp_in, gate_up[:, 1, :].T, preferred_element_type=jnp.float32)
        act = (jax.nn.silu(gate) * upper).astype(jnp.bfloat16)
        mlp_out = jnp.dot(act, down_weight, preferred_element_type=jnp.float32)
        return ((resid + mlp_out).astype(jnp.bfloat16), cache)
    outputs, caches = lax.map(one_group, (packed, lengths, page_table))
    layer_out = outputs.reshape(TOKENS, D)
    kv_cache = jnp.transpose(caches, (1, 0, 2, 3, 4, 5)).reshape(2, GROUPS * PAGES, PAGE, KV, HD)
    return (layer_out, kv_cache)
```

```python
import math

import jax
import jax.numpy as jnp
from jax import lax
from jax.experimental import pallas as pl
from jax.experimental.pallas import tpu as pltpu
from jax.sharding import PartitionSpec as P

rope_theta = 1000000.0
norm_eps = 1e-06
MESH = pl.DeviceIdType.MESH


def from_partner(value, axis, bit):
    mask = 2**bit
    pairs = [(source, source ^ mask) for source in range(lax.axis_size(axis))]
    return lax.ppermute(value, axis, pairs)


def rms_scale(values, gain):
    mean_sq = jnp.mean(values * values, axis=-1, keepdims=True)
    return values * lax.rsqrt(mean_sq + norm_eps) * gain


def positions_of(lengths, slots):
    ends = jnp.cumsum(lengths)
    slot_ids = jnp.arange(slots, dtype=jnp.int32)
    passed = (ends[None, :] <= slot_ids[:, None]).astype(jnp.int32)
    segment = jnp.sum(passed, axis=1)
    start = jnp.sum(passed * lengths[None, :], axis=1)
    return (slot_ids, segment, slot_ids - start)


def rotate(values, position, head_dim):
    half = head_dim // 2
    freq = rope_theta ** (-(2.0 * jnp.arange(half, dtype=jnp.float32)) / head_dim)
    angle = position.astype(jnp.float32)[:, None] * freq[None, :]
    shape = (angle.shape[0],) + (1,) * (values.ndim - 2) + (half,)
    cosine = jnp.cos(angle).reshape(shape)
    sine = jnp.sin(angle).reshape(shape)
    first = values[..., :half]
    second = values[..., half:]
    return jnp.concatenate(
        [first * cosine - second * sine, second * cosine + first * sine], axis=-1
    )


def exchange_kernel(
    partial_ref,
    mine_ref,
    norm_ref,
    gate_ref,
    up_ref,
    down_ref,
    out_ref,
    acc,
    rows_in,
    resid,
    pooled,
    sums,
    from_first,
    from_second,
    from_chain,
    attn_send,
    attn_recv,
    chain_send,
    chain_recv,
    near_send,
    near_recv,
    far_send,
    far_recv,
    first_send,
    first_recv,
    second_send,
    second_recv,
    back_send,
    back_recv,
):
    req = lax.axis_index("req")
    z = lax.axis_index("mlp")
    depth = lax.axis_size("mlp")
    owned, _ = mine_ref.shape
    half = owned // 2
    group = 2 * depth * half
    x_bit = (req // 2) % 2
    y_bit = (req // 4) % 2
    here = y_bit * 2 + x_bit
    across_x = y_bit * 2 + 1 - x_bit
    across_y = (1 - y_bit) * 2 + x_bit
    across_both = (1 - y_bit) * 2 + 1 - x_bit
    x_device = (req + 2 * (1 - 2 * x_bit), z)
    y_device = (req + 4 * (1 - 2 * y_bit), z)
    near = ((across_x, x_device), (across_y, y_device))
    far = ((across_y, y_device), (across_x, x_device))
    z_device = ((req, z + 1), (req, z - 1))
    has_z = (z < depth - 1, z > 0)

    barrier = pltpu.get_barrier_semaphore()
    for device in (x_device, y_device):
        pl.semaphore_signal(barrier, inc=1, device_id=device, device_id_type=MESH)
    for way in range(2):

        @pl.when(has_z[way])
        def _():
            pl.semaphore_signal(barrier, inc=1, device_id=z_device[way], device_id_type=MESH)

    peers = 2 + has_z[0].astype(jnp.int32) + has_z[1].astype(jnp.int32)
    pl.semaphore_wait(barrier, peers)

    def remote(source, target, send, recv, device):
        return pltpu.make_async_remote_copy(
            src_ref=source,
            dst_ref=target,
            send_sem=send,
            recv_sem=recv,
            device_id=device,
            device_id_type=MESH,
        )

    def block(which, h, j):
        return pl.ds(pl.multiple_of(((which * 2 + h) * depth + j) * half, half), half)

    def at_distance(step, body):
        for way in range(2 if step else 1):
            j = z + step if way == 0 else z - step
            if step == 0:
                body(j, way)
            else:
                inside = j < depth if way == 0 else j >= 0

                @pl.when(inside)
                def _():
                    body(j, way)

    def attn_copy(j, way):
        return remote(
            acc.at[j], rows_in.at[way, j], attn_send.at[way, j], attn_recv.at[way, j], z_device[way]
        )

    def own_part(j):
        return partial_ref[pl.ds(pl.multiple_of(j * owned, owned), owned), :].astype(jnp.float32)

    def attn_step(j, way):
        upstream = has_z[1 - way]

        @pl.when(upstream)
        def _():
            attn_copy(j, way).wait_recv()
            acc[j] = (own_part(j) + rows_in[way, j].astype(jnp.float32)).astype(acc.dtype)

        @pl.when(jnp.logical_not(upstream))
        def _():
            acc[j] = partial_ref[pl.ds(pl.multiple_of(j * owned, owned), owned), :]

        attn_copy(j, way).start()

    for step in range(depth - 1, 0, -1):
        at_distance(step, attn_step)
    resid[...] = mine_ref[...].astype(jnp.float32) + own_part(z)
    for way in range(2):

        @pl.when(has_z[1 - way])
        def _():
            attn_copy(z, way).wait_recv()
            resid[...] += rows_in[way, z].astype(jnp.float32)

    for h in range(2):
        value = resid[pl.ds(h * half, half), :]
        mean_sq = jnp.mean(value * value, axis=-1, keepdims=True)
        normed = value * lax.rsqrt(mean_sq + norm_eps) * norm_ref[...]
        pooled[block(here, h, z), :] = normed.astype(pooled.dtype)

    def chain_copy(h, j, way):
        rows = pooled.at[block(here, h, j), :]
        return remote(rows, rows, chain_send.at[way, h, j], chain_recv.at[h, j], z_device[way])

    def near_copy(h, j, arriving=False):
        rows = pooled.at[block(near[h][0] if arriving else here, h, j), :]
        return remote(rows, rows, near_send.at[h, j], near_recv.at[h, j], near[h][1])

    def far_copy(h, k, j):
        rows = pooled.at[block((here, near[h][0])[k], h, j), :]
        return remote(rows, rows, far_send.at[h, k, j], far_recv.at[h, k, j], far[h][1])

    def gather_step(step):
        def body(j, way):
            for h in range(2):
                if step > 0:
                    chain_copy(h, j, 1 - way).wait_recv()
                for onward in range(2) if step == 0 else (1 - way,):

                    @pl.when(has_z[onward])
                    def _():
                        chain_copy(h, j, onward).start()

                near_copy(h, j).start()
            for h in range(2):
                far_copy(h, 0, j).start()

        return body

    def forward(j, way):
        for h in range(2):
            near_copy(h, j, True).wait_recv()
            far_copy(h, 1, j).start()

    for step in range(depth):
        at_distance(step, gather_step(step))
        if step > 0:
            at_distance(step - 1, forward)
    at_distance(depth - 1, forward)

    def first_copy(h, k, j):
        source = (far[h][0], across_both)[k]
        return remote(
            sums.at[block(source, h, j), :],
            from_first.at[h, k, j],
            first_send.at[h, k, j],
            first_recv.at[h, k, j],
            far[h][1],
        )

    def second_copy(h, j):
        return remote(
            sums.at[block(near[h][0], h, j), :],
            from_second.at[h, j],
            second_send.at[h, j],
            second_recv.at[h, j],
            near[h][1],
        )

    def back_copy(h, j, way):
        return remote(
            sums.at[block(here, h, j), :],
            from_chain.at[way, h, j],
            back_send.at[way, h, j],
            back_recv.at[way, h, j],
            z_device[way],
        )

    halves_in = ((), ((1, 0),), ((0, 0),), ((0, 1), (1, 1)))

    def one_pack(i, carry):
        x_of = (x_bit + i % 2) % 2
        y_of = (y_bit + i // 2) % 2
        which = y_of * 2 + x_of
        for place in range(1, 4):

            @pl.when(i == place)
            def _():
                for h, k in halves_in[place]:
                    for j in range(depth):
                        far_copy(h, k, j).wait_recv()

        rows = pl.ds(pl.multiple_of(which * group, group), group)
        value = pooled[rows, :]
        dims = (((1,), (1,)), ((), ()))
        gate = lax.dot_general(value, gate_ref[...], dims, preferred_element_type=jnp.float32)
        upper = lax.dot_general(value, up_ref[...], dims, preferred_element_type=jnp.float32)
        act = (gate / (1.0 + jnp.exp(-gate)) * upper).astype(jnp.bfloat16)
        sums[rows, :] = jnp.dot(act, down_ref[...], preferred_element_type=jnp.float32).astype(
            sums.dtype
        )
        for place in range(1, 4):

            @pl.when(i == place)
            def _():
                for step in range(depth - 1, -1, -1):

                    def body(j, way):
                        for h, k in halves_in[place]:
                            first_copy(h, k, j).start()

                    at_distance(step, body)

        return carry

    lax.fori_loop(0, 4, one_pack, 0)

    def second_step(j, way):
        for h in range(2):
            first_copy(h, 1, j).wait_recv()
            rows = block(near[h][0], h, j)
            total = sums[rows, :].astype(jnp.float32) + from_first[h, 1, j].astype(jnp.float32)
            sums[rows, :] = total.astype(sums.dtype)
            second_copy(h, j).start()

    def all_here(h, j):
        first_copy(h, 0, j).wait_recv()
        second_copy(h, j).wait_recv()
        return (
            sums[block(here, h, j), :].astype(jnp.float32)
            + from_first[h, 0, j].astype(jnp.float32)
            + from_second[h, j].astype(jnp.float32)
        )

    def back_step(j, way):
        for h in range(2):
            rows = block(here, h, j)
            total = all_here(h, j)
            upstream = has_z[1 - way]

            @pl.when(upstream)
            def _():
                back_copy(h, j, way).wait_recv()
                sums[rows, :] = (total + from_chain[way, h, j].astype(jnp.float32)).astype(
                    sums.dtype
                )

            @pl.when(jnp.logical_not(upstream))
            def _():
                sums[rows, :] = total.astype(sums.dtype)

            back_copy(h, j, way).start()

    for step in range(depth - 1, -1, -1):
        at_distance(step, second_step)
        if step < depth - 1:
            at_distance(step + 1, back_step)
    for h in range(2):
        rows = pl.ds(h * half, half)
        resid[rows, :] += all_here(h, z)
        for way in range(2):

            @pl.when(has_z[1 - way])
            def _():
                back_copy(h, z, way).wait_recv()
                resid[rows, :] += from_chain[way, h, z].astype(jnp.float32)

        out_ref[rows, :] = resid[rows, :].astype(out_ref.dtype)

    def sent_step(step):
        def body(j, way):
            if step > 0:
                attn_copy(j, way).wait_send()
            for h in range(2):
                for onward in range(2) if step == 0 else (1 - way,):

                    @pl.when(has_z[onward])
                    def _():
                        chain_copy(h, j, onward).wait_send()

                if step > 0:
                    back_copy(h, j, way).wait_send()

        return body

    for step in range(depth):
        at_distance(step, sent_step(step))
    for h in range(2):
        for j in range(depth):
            near_copy(h, j).wait_send()
            second_copy(h, j).wait_send()
            for k in range(2):
                far_copy(h, k, j).wait_send()
                first_copy(h, k, j).wait_send()


def exchange(partial, mine, norm, gate, up, down):
    depth = lax.axis_size("mlp")
    owned, width = mine.shape
    half = owned // 2
    pool = 4 * depth * owned
    dma = pltpu.SemaphoreType.DMA
    low = jnp.bfloat16
    flops = 6 * pool * width * gate.shape[0]
    return pl.pallas_call(
        exchange_kernel,
        out_shape=jax.ShapeDtypeStruct((owned, width), low),
        in_specs=[pl.BlockSpec(memory_space=pltpu.VMEM)] * 6,
        out_specs=pl.BlockSpec(memory_space=pltpu.VMEM),
        scratch_shapes=[
            pltpu.VMEM((depth, owned, width), low),
            pltpu.VMEM((2, depth, owned, width), low),
            pltpu.VMEM((owned, width), jnp.float32),
            pltpu.VMEM((pool, width), low),
            pltpu.VMEM((pool, width), low),
            pltpu.VMEM((2, 2, depth, half, width), low),
            pltpu.VMEM((2, depth, half, width), low),
            pltpu.VMEM((2, 2, depth, half, width), low),
            dma((2, depth)),
            dma((2, depth)),
            dma((2, 2, depth)),
            dma((2, depth)),
            dma((2, depth)),
            dma((2, depth)),
            dma((2, 2, depth)),
            dma((2, 2, depth)),
            dma((2, 2, depth)),
            dma((2, 2, depth)),
            dma((2, depth)),
            dma((2, depth)),
            dma((2, 2, depth)),
            dma((2, 2, depth)),
        ],
        cost_estimate=pl.CostEstimate(
            flops=flops, bytes_accessed=6 * gate.shape[0] * width, transcendentals=0
        ),
        compiler_params=pltpu.CompilerParams(
            collective_id=0, has_side_effects=True, vmem_limit_bytes=52 * 1024 * 1024
        ),
    )(partial, mine, norm.reshape(1, width), gate, up, down)


def per_device(
    tokens,
    lengths,
    page_table,
    attn_norm,
    qkv_weight,
    q_norm,
    k_norm,
    o_weight,
    mlp_norm,
    gate_up,
    down_weight,
):
    slots = tokens.shape[0]
    head_dim = q_norm.shape[0]
    local_kv = qkv_weight.shape[1]
    group_q = qkv_weight.shape[2] // head_dim - 2
    pages = page_table.shape[1]
    page_rows = slots // pages
    owned = slots // lax.axis_size("mlp")
    slot_ids, segment, position = positions_of(lengths[0], slots)
    normed = rms_scale(tokens.astype(jnp.float32), attn_norm).astype(jnp.bfloat16)
    qkv = jnp.einsum("sd,dkc->skc", normed, qkv_weight, preferred_element_type=jnp.float32)
    query = qkv[:, :, : group_q * head_dim].reshape(slots, local_kv, group_q, head_dim)
    key = qkv[:, :, group_q * head_dim : (group_q + 1) * head_dim]
    value = qkv[:, :, (group_q + 1) * head_dim :]
    query = rotate(rms_scale(query, q_norm), position, head_dim).astype(jnp.bfloat16)
    key = rotate(rms_scale(key, k_norm), position, head_dim).astype(jnp.bfloat16)
    value = value.astype(jnp.bfloat16)
    key_pages = key.reshape(pages, page_rows, local_kv, head_dim)
    value_pages = value.reshape(pages, page_rows, local_kv, head_dim)
    kv_cache = jnp.zeros((2, pages, page_rows, local_kv, head_dim), jnp.bfloat16)
    kv_cache = kv_cache.at[:, page_table[0]].set(jnp.stack([key_pages, value_pages]))
    scores = jnp.einsum(
        "skgd,tkd->kgst", query, key, preferred_element_type=jnp.float32
    ) / math.sqrt(head_dim)
    allowed = (segment[:, None] == segment[None, :]) & (slot_ids[None, :] <= slot_ids[:, None])
    weights = jnp.where(allowed, jnp.exp(scores), 0.0)
    probs = (weights / jnp.sum(weights, axis=-1, keepdims=True)).astype(jnp.bfloat16)
    context = jnp.einsum("kgst,tkd->skgd", probs, value, preferred_element_type=jnp.float32)
    context = context.astype(jnp.bfloat16).reshape(slots, local_kv * group_q * head_dim)
    partial = jnp.dot(context, o_weight, preferred_element_type=jnp.float32).astype(jnp.bfloat16)
    mine = lax.dynamic_slice_in_dim(tokens, lax.axis_index("mlp") * owned, owned, 0)
    req_bits = lax.axis_size("req").bit_length() - 1
    units = [gate_up[:, 0, :], gate_up[:, 1, :], down_weight]
    for bit in (0, *range(3, req_bits)):
        units = [jnp.concatenate([part, from_partner(part, "req", bit)], axis=0) for part in units]
    layer_out = exchange(partial, mine, mlp_norm, *units)
    return (layer_out, kv_cache)


def solution(mesh):
    return jax.shard_map(
        per_device,
        mesh=mesh,
        in_specs=(
            P("req", None),
            P("req", None),
            P("req", None),
            P(),
            P(None, "mlp", None),
            P(),
            P(),
            P("mlp", None),
            P(),
            P(("req", "mlp"), None, None),
            P(("req", "mlp"), None),
        ),
        out_specs=(P(("req", "mlp"), None), P(None, "req", None, "mlp", None)),
        check_vma=False,
    )
```

```python
import math

import jax
import jax.numpy as jnp
from jax import lax
from jax.experimental import pallas as pl
from jax.experimental.pallas import tpu as pltpu
from jax.sharding import PartitionSpec as P

rope_theta = 1000000.0
norm_eps = 1e-06
MESH = pl.DeviceIdType.MESH


def from_partner(value, axis, bit):
    mask = 2**bit
    pairs = [(source, source ^ mask) for source in range(lax.axis_size(axis))]
    return lax.ppermute(value, axis, pairs)


def rms_scale(values, gain):
    mean_sq = jnp.mean(values * values, axis=-1, keepdims=True)
    return values * lax.rsqrt(mean_sq + norm_eps) * gain


def positions_of(lengths, slots):
    ends = jnp.cumsum(lengths)
    slot_ids = jnp.arange(slots, dtype=jnp.int32)
    passed = (ends[None, :] <= slot_ids[:, None]).astype(jnp.int32)
    segment = jnp.sum(passed, axis=1)
    start = jnp.sum(passed * lengths[None, :], axis=1)
    return (slot_ids, segment, slot_ids - start)


def rotate(values, position, head_dim):
    half = head_dim // 2
    freq = rope_theta ** (-(2.0 * jnp.arange(half, dtype=jnp.float32)) / head_dim)
    angle = position.astype(jnp.float32)[:, None] * freq[None, :]
    shape = (angle.shape[0],) + (1,) * (values.ndim - 2) + (half,)
    cosine = jnp.cos(angle).reshape(shape)
    sine = jnp.sin(angle).reshape(shape)
    first = values[..., :half]
    second = values[..., half:]
    return jnp.concatenate(
        [first * cosine - second * sine, second * cosine + first * sine], axis=-1
    )


def exchange_kernel(
    partial_ref,
    mine_ref,
    norm_ref,
    pairs_ref,
    far_pairs_ref,
    down_own_ref,
    far_down_ref,
    out_ref,
    gate_ref,
    up_ref,
    down_ref,
    acc,
    rows_in,
    resid,
    pooled,
    sums,
    from_first,
    from_second,
    from_chain,
    attn_send,
    attn_recv,
    chain_send,
    chain_recv,
    near_send,
    near_recv,
    far_send,
    far_recv,
    first_send,
    first_recv,
    second_send,
    second_recv,
    back_send,
    back_recv,
    unit_sem,
):
    req = lax.axis_index("req")
    z = lax.axis_index("mlp")
    depth = lax.axis_size("mlp")
    owned, _ = mine_ref.shape
    half = owned // 2
    group = 2 * depth * half
    x_bit = (req // 2) % 2
    y_bit = (req // 4) % 2
    here = y_bit * 2 + x_bit
    across_x = y_bit * 2 + 1 - x_bit
    across_y = (1 - y_bit) * 2 + x_bit
    across_both = (1 - y_bit) * 2 + 1 - x_bit
    x_device = (req + 2 * (1 - 2 * x_bit), z)
    y_device = (req + 4 * (1 - 2 * y_bit), z)
    near = ((across_x, x_device), (across_y, y_device))
    far = ((across_y, y_device), (across_x, x_device))
    z_device = ((req, z + 1), (req, z - 1))
    has_z = (z < depth - 1, z > 0)

    barrier = pltpu.get_barrier_semaphore()
    for device in (x_device, y_device):
        pl.semaphore_signal(barrier, inc=1, device_id=device, device_id_type=MESH)
    for way in range(2):

        @pl.when(has_z[way])
        def _():
            pl.semaphore_signal(barrier, inc=1, device_id=z_device[way], device_id_type=MESH)

    peers = 2 + has_z[0].astype(jnp.int32) + has_z[1].astype(jnp.int32)
    pl.semaphore_wait(barrier, peers)

    count = down_own_ref.shape[0]
    unit_copies = []
    for side, (pairs, down) in enumerate(
        ((pairs_ref, down_own_ref), (far_pairs_ref, far_down_ref))
    ):
        place = pl.ds(side * count, count)
        for k, (source, target) in enumerate(
            ((pairs.at[0], gate_ref), (pairs.at[1], up_ref), (down, down_ref))
        ):
            unit_copies.append(
                pltpu.make_async_copy(source, target.at[place, :], unit_sem.at[side, k])
            )
    for copy in unit_copies:
        copy.start()

    def remote(source, target, send, recv, device):
        return pltpu.make_async_remote_copy(
            src_ref=source,
            dst_ref=target,
            send_sem=send,
            recv_sem=recv,
            device_id=device,
            device_id_type=MESH,
        )

    def block(which, h, j):
        return pl.ds(pl.multiple_of(((which * 2 + h) * depth + j) * half, half), half)

    def at_distance(step, body):
        for way in range(2 if step else 1):
            j = z + step if way == 0 else z - step
            if step == 0:
                body(j, way)
            else:
                inside = j < depth if way == 0 else j >= 0

                @pl.when(inside)
                def _():
                    body(j, way)

    def attn_copy(j, way):
        return remote(
            acc.at[j], rows_in.at[way, j], attn_send.at[way, j], attn_recv.at[way, j], z_device[way]
        )

    def own_part(j):
        return partial_ref[pl.ds(pl.multiple_of(j * owned, owned), owned), :].astype(jnp.float32)

    def attn_step(j, way):
        upstream = has_z[1 - way]

        @pl.when(upstream)
        def _():
            attn_copy(j, way).wait_recv()
            acc[j] = (own_part(j) + rows_in[way, j].astype(jnp.float32)).astype(acc.dtype)

        @pl.when(jnp.logical_not(upstream))
        def _():
            acc[j] = partial_ref[pl.ds(pl.multiple_of(j * owned, owned), owned), :]

        attn_copy(j, way).start()

    for step in range(depth - 1, 0, -1):
        at_distance(step, attn_step)
    resid[...] = mine_ref[...].astype(jnp.float32) + own_part(z)
    for way in range(2):

        @pl.when(has_z[1 - way])
        def _():
            attn_copy(z, way).wait_recv()
            resid[...] += rows_in[way, z].astype(jnp.float32)

    for h in range(2):
        value = resid[pl.ds(h * half, half), :]
        mean_sq = jnp.mean(value * value, axis=-1, keepdims=True)
        normed = value * lax.rsqrt(mean_sq + norm_eps) * norm_ref[...]
        pooled[block(here, h, z), :] = normed.astype(pooled.dtype)

    def chain_copy(h, j, way):
        rows = pooled.at[block(here, h, j), :]
        return remote(rows, rows, chain_send.at[way, h, j], chain_recv.at[h, j], z_device[way])

    def near_copy(h, j, arriving=False):
        rows = pooled.at[block(near[h][0] if arriving else here, h, j), :]
        return remote(rows, rows, near_send.at[h, j], near_recv.at[h, j], near[h][1])

    def far_copy(h, k, j):
        rows = pooled.at[block((here, near[h][0])[k], h, j), :]
        return remote(rows, rows, far_send.at[h, k, j], far_recv.at[h, k, j], far[h][1])

    def gather_step(step):
        def body(j, way):
            for h in range(2):
                if step > 0:
                    chain_copy(h, j, 1 - way).wait_recv()
                for onward in range(2) if step == 0 else (1 - way,):

                    @pl.when(has_z[onward])
                    def _():
                        chain_copy(h, j, onward).start()

                near_copy(h, j).start()
            for h in range(2):
                far_copy(h, 0, j).start()

        return body

    def forward(j, way):
        for h in range(2):
            near_copy(h, j, True).wait_recv()
            far_copy(h, 1, j).start()

    for step in range(depth):
        at_distance(step, gather_step(step))
        if step > 0:
            at_distance(step - 1, forward)
    at_distance(depth - 1, forward)

    def first_copy(h, k, j):
        source = (far[h][0], across_both)[k]
        return remote(
            sums.at[block(source, h, j), :],
            from_first.at[h, k, j],
            first_send.at[h, k, j],
            first_recv.at[h, k, j],
            far[h][1],
        )

    def second_copy(h, j):
        return remote(
            sums.at[block(near[h][0], h, j), :],
            from_second.at[h, j],
            second_send.at[h, j],
            second_recv.at[h, j],
            near[h][1],
        )

    def back_copy(h, j, way):
        return remote(
            sums.at[block(here, h, j), :],
            from_chain.at[way, h, j],
            back_send.at[way, h, j],
            back_recv.at[way, h, j],
            z_device[way],
        )

    halves_in = ((), ((1, 0),), ((0, 0),), ((0, 1), (1, 1)))

    def one_pack(i, carry):
        x_of = (x_bit + i % 2) % 2
        y_of = (y_bit + i // 2) % 2
        which = y_of * 2 + x_of
        for place in range(1, 4):

            @pl.when(i == place)
            def _():
                for h, k in halves_in[place]:
                    for j in range(depth):
                        far_copy(h, k, j).wait_recv()

        rows = pl.ds(pl.multiple_of(which * group, group), group)
        value = pooled[rows, :]
        dims = (((1,), (1,)), ((), ()))
        gate = lax.dot_general(value, gate_ref[...], dims, preferred_element_type=jnp.float32)
        upper = lax.dot_general(value, up_ref[...], dims, preferred_element_type=jnp.float32)
        act = (gate / (1.0 + jnp.exp(-gate)) * upper).astype(jnp.bfloat16)
        sums[rows, :] = jnp.dot(act, down_ref[...], preferred_element_type=jnp.float32).astype(
            sums.dtype
        )
        for place in range(1, 4):

            @pl.when(i == place)
            def _():
                for step in range(depth - 1, -1, -1):

                    def body(j, way):
                        for h, k in halves_in[place]:
                            first_copy(h, k, j).start()

                    at_distance(step, body)

        return carry

    for copy in unit_copies:
        copy.wait()
    lax.fori_loop(0, 4, one_pack, 0)

    def second_step(j, way):
        for h in range(2):
            first_copy(h, 1, j).wait_recv()
            rows = block(near[h][0], h, j)
            total = sums[rows, :].astype(jnp.float32) + from_first[h, 1, j].astype(jnp.float32)
            sums[rows, :] = total.astype(sums.dtype)
            second_copy(h, j).start()

    def all_here(h, j):
        first_copy(h, 0, j).wait_recv()
        second_copy(h, j).wait_recv()
        return (
            sums[block(here, h, j), :].astype(jnp.float32)
            + from_first[h, 0, j].astype(jnp.float32)
            + from_second[h, j].astype(jnp.float32)
        )

    def back_step(j, way):
        for h in range(2):
            rows = block(here, h, j)
            total = all_here(h, j)
            upstream = has_z[1 - way]

            @pl.when(upstream)
            def _():
                back_copy(h, j, way).wait_recv()
                sums[rows, :] = (total + from_chain[way, h, j].astype(jnp.float32)).astype(
                    sums.dtype
                )

            @pl.when(jnp.logical_not(upstream))
            def _():
                sums[rows, :] = total.astype(sums.dtype)

            back_copy(h, j, way).start()

    for step in range(depth - 1, -1, -1):
        at_distance(step, second_step)
        if step < depth - 1:
            at_distance(step + 1, back_step)
    for h in range(2):
        rows = pl.ds(h * half, half)
        resid[rows, :] += all_here(h, z)
        for way in range(2):

            @pl.when(has_z[1 - way])
            def _():
                back_copy(h, z, way).wait_recv()
                resid[rows, :] += from_chain[way, h, z].astype(jnp.float32)

        out_ref[rows, :] = resid[rows, :].astype(out_ref.dtype)

    def sent_step(step):
        def body(j, way):
            if step > 0:
                attn_copy(j, way).wait_send()
            for h in range(2):
                for onward in range(2) if step == 0 else (1 - way,):

                    @pl.when(has_z[onward])
                    def _():
                        chain_copy(h, j, onward).wait_send()

                if step > 0:
                    back_copy(h, j, way).wait_send()

        return body

    for step in range(depth):
        at_distance(step, sent_step(step))
    for h in range(2):
        for j in range(depth):
            near_copy(h, j).wait_send()
            second_copy(h, j).wait_send()
            for k in range(2):
                far_copy(h, k, j).wait_send()
                first_copy(h, k, j).wait_send()


def exchange(partial, mine, norm, pairs, far_pairs, down, far_down):
    depth = lax.axis_size("mlp")
    owned, width = mine.shape
    half = owned // 2
    pool = 4 * depth * owned
    dma = pltpu.SemaphoreType.DMA
    low = jnp.bfloat16
    units = 2 * down.shape[0]
    flops = 6 * pool * width * units
    return pl.pallas_call(
        exchange_kernel,
        out_shape=jax.ShapeDtypeStruct((owned, width), low),
        in_specs=[pl.BlockSpec(memory_space=pltpu.VMEM)] * 3
        + [pl.BlockSpec(memory_space=pl.ANY)] * 4,
        out_specs=pl.BlockSpec(memory_space=pltpu.VMEM),
        scratch_shapes=[
            pltpu.VMEM((units, width), low),
            pltpu.VMEM((units, width), low),
            pltpu.VMEM((units, width), low),
            pltpu.VMEM((depth, owned, width), low),
            pltpu.VMEM((2, depth, owned, width), low),
            pltpu.VMEM((owned, width), jnp.float32),
            pltpu.VMEM((pool, width), low),
            pltpu.VMEM((pool, width), low),
            pltpu.VMEM((2, 2, depth, half, width), low),
            pltpu.VMEM((2, depth, half, width), low),
            pltpu.VMEM((2, 2, depth, half, width), low),
            dma((2, depth)),
            dma((2, depth)),
            dma((2, 2, depth)),
            dma((2, depth)),
            dma((2, depth)),
            dma((2, depth)),
            dma((2, 2, depth)),
            dma((2, 2, depth)),
            dma((2, 2, depth)),
            dma((2, 2, depth)),
            dma((2, depth)),
            dma((2, depth)),
            dma((2, 2, depth)),
            dma((2, 2, depth)),
            dma((2, 3)),
        ],
        cost_estimate=pl.CostEstimate(
            flops=flops, bytes_accessed=6 * units * width, transcendentals=0
        ),
        compiler_params=pltpu.CompilerParams(
            collective_id=0, has_side_effects=True, vmem_limit_bytes=52 * 1024 * 1024
        ),
    )(partial, mine, norm.reshape(1, width), pairs, far_pairs, down, far_down)


def per_device(
    tokens,
    lengths,
    page_table,
    attn_norm,
    qkv_weight,
    q_norm,
    k_norm,
    o_weight,
    mlp_norm,
    gate_up,
    down_weight,
):
    slots = tokens.shape[0]
    head_dim = q_norm.shape[0]
    local_kv = qkv_weight.shape[1]
    group_q = qkv_weight.shape[2] // head_dim - 2
    pages = page_table.shape[1]
    page_rows = slots // pages
    owned = slots // lax.axis_size("mlp")
    slot_ids, segment, position = positions_of(lengths[0], slots)
    normed = rms_scale(tokens.astype(jnp.float32), attn_norm).astype(jnp.bfloat16)
    qkv = jnp.einsum("sd,dkc->skc", normed, qkv_weight, preferred_element_type=jnp.float32)
    query = qkv[:, :, : group_q * head_dim].reshape(slots, local_kv, group_q, head_dim)
    key = qkv[:, :, group_q * head_dim : (group_q + 1) * head_dim]
    value = qkv[:, :, (group_q + 1) * head_dim :]
    query = rotate(rms_scale(query, q_norm), position, head_dim).astype(jnp.bfloat16)
    key = rotate(rms_scale(key, k_norm), position, head_dim).astype(jnp.bfloat16)
    value = value.astype(jnp.bfloat16)
    key_pages = key.reshape(pages, page_rows, local_kv, head_dim)
    value_pages = value.reshape(pages, page_rows, local_kv, head_dim)
    kv_cache = jnp.zeros((2, pages, page_rows, local_kv, head_dim), jnp.bfloat16)
    kv_cache = kv_cache.at[:, page_table[0]].set(jnp.stack([key_pages, value_pages]))
    scores = jnp.einsum(
        "skgd,tkd->kgst", query, key, preferred_element_type=jnp.float32
    ) / math.sqrt(head_dim)
    allowed = (segment[:, None] == segment[None, :]) & (slot_ids[None, :] <= slot_ids[:, None])
    weights = jnp.where(allowed, jnp.exp(scores), 0.0)
    probs = (weights / jnp.sum(weights, axis=-1, keepdims=True)).astype(jnp.bfloat16)
    context = jnp.einsum("kgst,tkd->skgd", probs, value, preferred_element_type=jnp.float32)
    context = context.astype(jnp.bfloat16).reshape(slots, local_kv * group_q * head_dim)
    partial = jnp.dot(context, o_weight, preferred_element_type=jnp.float32).astype(jnp.bfloat16)
    mine = lax.dynamic_slice_in_dim(tokens, lax.axis_index("mlp") * owned, owned, 0)
    req_bits = lax.axis_size("req").bit_length() - 1
    pairs = lax.optimization_barrier(jnp.transpose(gate_up, (1, 0, 2)))
    down = down_weight
    for bit in range(3, req_bits):
        pairs = jnp.concatenate([pairs, from_partner(pairs, "req", bit)], axis=1)
        down = jnp.concatenate([down, from_partner(down, "req", bit)], axis=0)
    far_pairs = from_partner(pairs, "req", 0)
    far_down = from_partner(down, "req", 0)
    layer_out = exchange(partial, mine, mlp_norm, pairs, far_pairs, down, far_down)
    return (layer_out, kv_cache)


def solution(mesh):
    return jax.shard_map(
        per_device,
        mesh=mesh,
        in_specs=(
            P("req", None),
            P("req", None),
            P("req", None),
            P(),
            P(None, "mlp", None),
            P(),
            P(),
            P("mlp", None),
            P(),
            P(("req", "mlp"), None, None),
            P(("req", "mlp"), None),
        ),
        out_specs=(P(("req", "mlp"), None), P(None, "req", None, "mlp", None)),
        check_vma=False,
    )
```
